128 devices in a mesh: seq: 16 (over x, y_lo, core), fsdp: 8 (over y_hi, z).
Axes of the slice: x: 4, y: 4 (y_hi: 2, y_lo: 2; y = y_hi * 2 + y_lo), z: 4, core: 2. Of those that a mesh axis runs over, the one named last changes fastest.
Arguments:
- block_in: float32 [8, 8192, 640], P('fsdp', 'seq'), may hold values from -6 to 6
- seg_ids: int32 [8, 8192], P('fsdp', 'seq'), may hold values from 0 to 2, as said below
- cotangent: float32 [8, 8192, 640], P('fsdp', 'seq'), may hold values from -6 to 6
- query_weight: float32 [640, 1024], P(('seq', 'fsdp')), may hold values from -0.25 to 0.25
- query_mean: float32 [640, 1024], P(('seq', 'fsdp')), may hold values from -160 to 160
- query_square: float32 [640, 1024], P(('seq', 'fsdp')), may hold values from 3276.8 to 26214.4
- keyval_weight: float32 [640, 512], P(('seq', 'fsdp')), may hold values from -0.25 to 0.25
- keyval_mean: float32 [640, 512], P(('seq', 'fsdp')), may hold values from -512 to 512
- keyval_square: float32 [640, 512], P(('seq', 'fsdp')), may hold values from 29491.2 to 235929.6
- output_weight: float32 [1024, 640], P(('seq', 'fsdp')), may hold values from -4 to 4
- output_mean: float32 [1024, 640], P(('seq', 'fsdp')), may hold values from -8 to 8
- output_square: float32 [1024, 640], P(('seq', 'fsdp')), may hold values from 8.192 to 65.536
- gateup_weight: float32 [640, 4096], P(('seq', 'fsdp')), may hold values from -0.25 to 0.25
- gateup_mean: float32 [640, 4096], P(('seq', 'fsdp')), may hold values from -56 to 56
- gateup_square: float32 [640, 4096], P(('seq', 'fsdp')), may hold values from 373.5552 to 3080.192
- down_weight: float32 [2048, 640], P(('seq', 'fsdp')), may hold values from -0.125 to 0.125
- down_mean: float32 [2048, 640], P(('seq', 'fsdp')), may hold values from -96 to 96
- down_square: float32 [2048, 640], P(('seq', 'fsdp')), may hold values from 1179.648 to 9437.184
- norm_gains: float32 [2, 640], P(None, ('seq', 'fsdp')), may hold values from 0.5 to 1.5
- gains_mean: float32 [2, 640], P(None, ('seq', 'fsdp')), may hold values from -320 to 320
- gains_square: float32 [2, 640], P(None, ('seq', 'fsdp')), may hold values from 13107.2 to 104857.6
Outputs:
- block_out: float32 [8, 8192, 640], P('fsdp', 'seq')
- input_grad: float32 [8, 8192, 640], P('fsdp', 'seq')
- query_mean_new: float32 [640, 1024], P(('seq', 'fsdp'))
- query_square_new: float32 [640, 1024], P(('seq', 'fsdp'))
- query_weight_new: float32 [640, 1024], P(('seq', 'fsdp'))
- keyval_mean_new: float32 [640, 512], P(('seq', 'fsdp'))
- keyval_square_new: float32 [640, 512], P(('seq', 'fsdp'))
- keyval_weight_new: float32 [640, 512], P(('seq', 'fsdp'))
- output_mean_new: float32 [1024, 640], P(('seq', 'fsdp'))
- output_square_new: float32 [1024, 640], P(('seq', 'fsdp'))
- output_weight_new: float32 [1024, 640], P(('seq', 'fsdp'))
- gateup_mean_new: float32 [640, 4096], P(('seq', 'fsdp'))
- gateup_square_new: float32 [640, 4096], P(('seq', 'fsdp'))
- gateup_weight_new: float32 [640, 4096], P(('seq', 'fsdp'))
- down_mean_new: float32 [2048, 640], P(('seq', 'fsdp'))
- down_square_new: float32 [2048, 640], P(('seq', 'fsdp'))
- down_weight_new: float32 [2048, 640], P(('seq', 'fsdp'))
- gains_mean_new: float32 [2, 640], P(None, ('seq', 'fsdp'))
- gains_square_new: float32 [2, 640], P(None, ('seq', 'fsdp'))
- norm_gains_new: float32 [2, 640], P(None, ('seq', 'fsdp'))
The draws below stay inside these ranges and needn't reach their ends.
Inputs may be any that keep to these rules, and one draw needn't show every extreme that they name: `seg_ids`: document numbers never fall along a sequence, and every sequence holds documents 0, 1 and 2.
All inputs are finite; a program needn't handle non-finite values.
Results may differ from the reference program's by a relative error of at most 0.015.
Values may be sent and summed in bfloat16 or wider, within the bound.
No kernel may reach another device: no remote copies, remote signals or barrier semaphores. Data moves between devices by JAX's collectives and lax.ppermute only.
A program may use at most 128 MiB of HBM per device.

```python
import math
import jax
import jax.numpy as jnp
from jax import lax

D = 640
HQ = 4
HD = 256
FF = 2048
WINDOW = 512
TOK_DEV = 512
STEP = 5
SEQS = 8
LENGTH = 8192
TOKENS = 65536


def draw_seg_ids(key, part):
    key = jax.random.fold_in(key, 11)
    first_key, last_key = jax.random.split(key)
    leading = jax.random.randint(first_key, (SEQS, 1), 1, TOK_DEV // 2 + 1)
    trailing = jax.random.randint(last_key, (SEQS, 1), 1, TOK_DEV // 2 + 1)
    places = jnp.arange(LENGTH, dtype=jnp.int32)[None, :]
    started = (places >= leading).astype(jnp.int32)
    ended = (places >= LENGTH - trailing).astype(jnp.int32)
    return (started + ended).astype(jnp.int32)


def block_scale(own_key, shape, pieces, least, largest):
    level = 1.0
    for dim, shards_of in pieces:
        heights = jax.random.uniform(jax.random.fold_in(jax.random.fold_in(own_key, 6), dim), (shards_of,), jnp.float32, least / len(pieces), largest / len(pieces))
        level = level * jnp.repeat(jnp.exp(heights), shape[dim] // shards_of).reshape((-1,) + (1,) * (len(shape) - 1 - dim))
    return level


def noise(key, dims, spread, most, shards=(), kind=jnp.bfloat16):
    entries = spread * jax.random.normal(key, dims, jnp.float32)
    if shards:
        entries = entries * block_scale(key, dims, shards, -0.22, 0.18)
    return jnp.clip(entries, -most, most).astype(kind)


def setup_inputs(seed: int = 0) -> dict:
    splits = jax.random.split(jax.random.key(seed), 22)
    return {
        "block_in": noise(splits[0], (SEQS, LENGTH, D), 1.0, 6.0, ((0, 8), (1, 16)), jnp.float32),
        "seg_ids": draw_seg_ids(jax.random.fold_in(splits[21], 71), 0),
        "cotangent": noise(splits[2], (SEQS, LENGTH, D), 1.0, 6.0, ((0, 8), (1, 16)), jnp.float32),
        "query_weight": noise(splits[3], (D, HQ * HD), D ** -0.5, 0.25, ((0, 128),), jnp.float32),
        "query_mean": noise(splits[4], (D, HQ * HD), (0.11 * TOKENS ** 0.5), 160.0, ((0, 128),), jnp.float32),
        "query_square": jnp.clip(jnp.exp(math.log(26214.4) - 2.0794415 * jax.random.uniform(splits[5], (D, HQ * HD), jnp.float32) ** block_scale(splits[5], (D, HQ * HD), ((0, 128),), -0.2, 0.2)), 3276.8, 26214.4),
        "keyval_weight": noise(splits[6], (D, 2 * HD), D ** -0.5, 0.25, ((0, 128),), jnp.float32),
        "keyval_mean": noise(splits[7], (D, 2 * HD), (0.33 * TOKENS ** 0.5), 512.0, ((0, 128),), jnp.float32),
        "keyval_square": jnp.clip(jnp.exp(math.log(235929.6) - 2.0794415 * jax.random.uniform(splits[8], (D, 2 * HD), jnp.float32) ** block_scale(splits[8], (D, 2 * HD), ((0, 128),), -0.2, 0.2)), 29491.2, 235929.6),
        "output_weight": noise(splits[9], (HQ * HD, D), (HQ * HD // WINDOW) ** -0.5, 4.0, ((0, 128),), jnp.float32),
        "output_mean": noise(splits[10], (HQ * HD, D), (0.0055 * TOKENS ** 0.5), 8.0, ((0, 128),), jnp.float32),
        "output_square": jnp.clip(jnp.exp(math.log(65.536) - 2.0794415 * jax.random.uniform(splits[11], (HQ * HD, D), jnp.float32) ** block_scale(splits[11], (HQ * HD, D), ((0, 128),), -0.2, 0.2)), 8.192, 65.536),
        "gateup_weight": noise(splits[12], (D, 2 * FF), D ** -0.5, 0.25, ((0, 128),), jnp.float32),
        "gateup_mean": noise(splits[13], (D, 2 * FF), (0.038 * TOKENS ** 0.5), 56.0, ((0, 128),), jnp.float32),
        "gateup_square": jnp.clip(jnp.exp(math.log(3080.192) - 2.1096814 * jax.random.uniform(splits[14], (D, 2 * FF), jnp.float32) ** block_scale(splits[14], (D, 2 * FF), ((0, 128),), -0.2, 0.2)), 373.5552, 3080.192),
        "down_weight": noise(splits[15], (FF, D), FF ** -0.5, 0.125, ((0, 128),), jnp.float32),
        "down_mean": noise(splits[16], (FF, D), (0.066 * TOKENS ** 0.5), 96.0, ((0, 128),), jnp.float32),
        "down_square": jnp.clip(jnp.exp(math.log(9437.184) - 2.0794415 * jax.random.uniform(splits[17], (FF, D), jnp.float32) ** block_scale(splits[17], (FF, D), ((0, 128),), -0.2, 0.2)), 1179.648, 9437.184),
        "norm_gains": jnp.clip(1.0 + 0.1 * jax.random.normal(splits[18], (2, D), jnp.float32), 0.5, 1.5),
        "gains_mean": noise(splits[19], (2, D), (0.22 * TOKENS ** 0.5), 320.0, ((1, 128),), jnp.float32),
        "gains_square": jnp.clip(jnp.exp(math.log(104857.6) - 2.0794415 * jax.random.uniform(splits[20], (2, D), jnp.float32) ** block_scale(splits[20], (2, D), ((1, 128),), -0.2, 0.2)), 13107.2, 104857.6),
    }


@jax.custom_vjp
def low(v):
    return lax.optimization_barrier(v.astype(jnp.bfloat16)).astype(jnp.float32)

@jax.custom_vjp
def low_back(v):
    return v

def low_keep(v):
    return (low(v), None)

def low_pass(kept, grad):
    return (grad,)

def back_keep(v):
    return (v, None)

def back_low(kept, grad):
    return (low(grad),)
low.defvjp(low_keep, low_pass)
low_back.defvjp(back_keep, back_low)
EPS_NORM = 1e-06
BETA_ONE = 0.9
BETA_TWO = 0.95
ADAM_EPS = 1e-08
DECAY = 0.1
GAIN_RATE = 0.5
RATE_FACTOR = 0.7
MASKED = -1e+30

def highest(left, right):
    return jnp.dot(left, right, precision=lax.Precision.HIGHEST, preferred_element_type=jnp.float32)

def rms_scale(values, gain):
    return values * lax.rsqrt(lax.optimization_barrier(jnp.mean(values * values, axis=-1, keepdims=True)) + EPS_NORM) * gain

def adamw_step(weight, mean_old, square_old, gradient, rate, decay):
    mean_new = BETA_ONE * mean_old + (1.0 - BETA_ONE) * gradient
    square_new = BETA_TWO * square_old + (1.0 - BETA_TWO) * gradient * gradient
    mean_hat = mean_new / (1.0 - BETA_ONE ** STEP)
    square_hat = square_new / (1.0 - BETA_TWO ** STEP)
    weight_new = weight - rate * (mean_hat / (jnp.sqrt(square_hat) + ADAM_EPS) + decay * weight)
    return (mean_new, square_new, weight_new)

def attend(queries, keys, values, seg_row):
    blocks = LENGTH // WINDOW
    scale = HD ** (-0.5)
    pad_keys = jnp.concatenate([jnp.zeros((WINDOW, HD), jnp.float32), keys], axis=0)
    pad_values = jnp.concatenate([jnp.zeros((WINDOW, HD), jnp.float32), values], axis=0)
    pad_ids = jnp.concatenate([jnp.full((WINDOW,), -1, jnp.int32), seg_row.astype(jnp.int32)], axis=0)
    offsets = jnp.arange(WINDOW, dtype=jnp.int32)[:, None] - jnp.arange(2 * WINDOW, dtype=jnp.int32)[None, :] + WINDOW
    nearby = (offsets >= 0) & (offsets < WINDOW)

    def one_block(index):
        start = (index * WINDOW).astype(jnp.int32)
        query_block = lax.dynamic_slice_in_dim(queries, start, WINDOW, 0).reshape(WINDOW, HQ, HD)
        key_block = lax.dynamic_slice_in_dim(pad_keys, start, 2 * WINDOW, 0)
        value_block = lax.dynamic_slice_in_dim(pad_values, start, 2 * WINDOW, 0)
        query_ids = lax.dynamic_slice_in_dim(seg_row.astype(jnp.int32), start, WINDOW, 0)
        key_ids = lax.dynamic_slice_in_dim(pad_ids, start, 2 * WINDOW, 0)
        allowed = nearby & (query_ids[:, None] == key_ids[None, :])
        raw = jnp.einsum('thd,jd->htj', query_block.astype(jnp.float32), key_block.astype(jnp.float32), precision=lax.Precision.HIGHEST) * scale
        scores = jnp.where(allowed[None], low_back(raw), MASKED)
        peak = lax.optimization_barrier(jnp.max(scores, axis=-1, keepdims=True))
        exponent = jnp.exp(scores - peak)
        probs = low(exponent / lax.optimization_barrier(jnp.sum(exponent, axis=-1, keepdims=True)))
        mixed = jnp.einsum('htj,jd->thd', probs.astype(jnp.float32), value_block.astype(jnp.float32), precision=lax.Precision.HIGHEST)
        return mixed.reshape(WINDOW, HQ * HD)
    outputs = lax.map(jax.checkpoint(one_block), jnp.arange(blocks, dtype=jnp.int32))
    return outputs.reshape(LENGTH, HQ * HD)

def layer(tokens_in, seg_row, query_w, keyval_w, output_w, gateup_w, down_w, gains):
    hidden_one = low(rms_scale(tokens_in, gains[0]))
    queries = low(low_back(highest(hidden_one, query_w)))
    keyvals = low(low_back(highest(hidden_one, keyval_w)))
    attended = low(low_back(attend(queries, keyvals[:, :HD], keyvals[:, HD:], seg_row)))
    middle = tokens_in + low_back(highest(attended, output_w))
    hidden_two = low(rms_scale(middle, gains[1]))
    gateup = low_back(highest(hidden_two, gateup_w))
    inner = low(jax.nn.gelu(gateup[:, :FF], approximate=True) * gateup[:, FF:])
    return middle + low_back(highest(inner, down_w))

def reference(block_in, seg_ids, cotangent, query_weight, query_mean, query_square, keyval_weight, keyval_mean, keyval_square, output_weight, output_mean, output_square, gateup_weight, gateup_mean, gateup_square, down_weight, down_mean, down_square, norm_gains, gains_mean, gains_square):

    def forward(tokens_all, query_w, keyval_w, output_w, gateup_w, down_w, gains):
        low_query = low(query_w)
        low_keyval = low(keyval_w)
        low_output = low(output_w)
        low_gateup = low(gateup_w)
        low_down = low(down_w)
        low_gains = low(gains)
        checked = jax.checkpoint(layer)

        def one_sequence(pair):
            return checked(pair[0], pair[1], low_query, low_keyval, low_output, low_gateup, low_down, low_gains)
        return lax.map(one_sequence, (tokens_all, seg_ids))
    block_out, pullback = jax.vjp(forward, block_in, query_weight, keyval_weight, output_weight, gateup_weight, down_weight, norm_gains)
    input_grad, query_sum, keyval_sum, output_sum, gateup_sum, down_sum, gains_sum = pullback(cotangent)
    query_new = adamw_step(query_weight, query_mean, query_square, query_sum, RATE_FACTOR * D ** (-0.5), DECAY)
    keyval_new = adamw_step(keyval_weight, keyval_mean, keyval_square, keyval_sum, RATE_FACTOR * D ** (-0.5), DECAY)
    output_new = adamw_step(output_weight, output_mean, output_square, output_sum, RATE_FACTOR * (HQ * HD // WINDOW) ** (-0.5), DECAY)
    gateup_new = adamw_step(gateup_weight, gateup_mean, gateup_square, gateup_sum, RATE_FACTOR * D ** (-0.5), DECAY)
    down_new = adamw_step(down_weight, down_mean, down_square, down_sum, RATE_FACTOR * FF ** (-0.5), DECAY)
    gains_new = adamw_step(norm_gains, gains_mean, gains_square, gains_sum, GAIN_RATE, 0.0)
    return (block_out, input_grad, query_new[0], query_new[1], query_new[2], keyval_new[0], keyval_new[1], keyval_new[2], output_new[0], output_new[1], output_new[2], gateup_new[0], gateup_new[1], gateup_new[2], down_new[0], down_new[1], down_new[2], gains_new[0], gains_new[1], gains_new[2])
```

```python
import functools

import jax
import jax.numpy as jnp
import numpy as np
from jax import lax
from jax.experimental import pallas as pl
from jax.experimental.pallas import tpu as pltpu
from jax.sharding import Mesh, PartitionSpec as P

D = 640
HQ = 4
HD = 256
FF = 2048
WINDOW = 512
STEP = 5
TOK = 512

EPS_NORM = 1e-06
BETA_ONE = 0.9
BETA_TWO = 0.95
ADAM_EPS = 1e-08
DECAY = 0.1
GAIN_RATE = 0.5
RATE_FACTOR = 0.7
MASKED = -1e30

SIZES = {"x": 4, "ylo": 2, "core": 2, "yhi": 2, "z": 4}
OWNERS = ("x", "ylo", "core", "yhi", "z")
SEQ = ("x", "ylo", "core")
FAR = ("x", "yhi", "ylo")
BF = jnp.bfloat16
F32 = jnp.float32

GU_ROWS = 16 * 40
DOWN_ROWS = 5 * 64
OUT_ROWS = 5 * 32
MLP_ROWS = GU_ROWS + DOWN_ROWS
ALL_ROWS = MLP_ROWS + OUT_ROWS
QKV_ROWS = 6 * 40
FIRST_ROWS = QKV_ROWS + 8
QO_ROWS = 160 + OUT_ROWS
KV_ROWS = 80 + 16
Z_GU = 16 * 160
Z_ROWS = Z_GU + 16 * 80
FAR_ROWS = 16 * 10 + 80
VMEM_LIMIT = 22 * 1024 * 1024
MLP_VMEM = 40 * 1024 * 1024
SCALE = HD ** (-0.5)


def dot(left, right):
    return jnp.dot(left, right, preferred_element_type=F32)


def product(form, left, right):
    return jnp.einsum(form, left, right, preferred_element_type=F32)


def adamw_step(weight, mean_old, square_old, gradient, rate, decay):
    mean_new = BETA_ONE * mean_old + (1.0 - BETA_ONE) * gradient
    square_new = BETA_TWO * square_old + (1.0 - BETA_TWO) * gradient * gradient
    mean_hat = mean_new / (1.0 - BETA_ONE**STEP)
    square_hat = square_new / (1.0 - BETA_TWO**STEP)
    weight_new = weight - rate * (mean_hat / (jnp.sqrt(square_hat) + ADAM_EPS) + decay * weight)
    return (mean_new, square_new, weight_new)


def other_core(value):
    return lax.ppermute(value, "core", [(0, 1), (1, 0)])


def by_core(own, other, axis):
    first = lax.axis_index("core") == 0
    return jnp.stack([jnp.where(first, own, other), jnp.where(first, other, own)], axis=axis)


def pick(value, index, axis):
    return lax.dynamic_index_in_dim(value, index, axis, keepdims=False)


def sent_z(value, step):
    return lax.ppermute(value, "z", [(i, (i + step) % 4) for i in range(4)])


def gathered_rows():
    natural = np.arange(D).reshape(4, 2, 2, 2, 4, 5)
    order = natural.transpose(0, 3, 1, 2, 4, 5).reshape(-1)
    out = np.zeros((D, D), np.float32)
    out[order, np.arange(D)] = 1.0
    return out


def gain_rows():
    k = np.arange(D)
    spread = (k[None, :] % 40 == np.arange(128)[:, None]).astype(np.float32)
    keep = (k[None, :] // 40 == np.arange(16)[:, None]).astype(np.float32)
    return spread, keep


def mm(left, right, dims):
    return lax.dot_general(left, right, (dims, ((), ())), preferred_element_type=F32)


NN = ((1,), (0,))
NT = ((1,), (1,))


def natural_columns(value, swap):
    high = value.astype(BF)
    low = (value - high.astype(F32)).astype(BF)
    return mm(high, swap, NT) + mm(low, swap, NT)


def norm_factor(value):
    return lax.rsqrt(jnp.mean(value * value, axis=-1, keepdims=True) + EPS_NORM)


def norm_back(back, value, gain):
    r = norm_factor(value)
    n = value * r
    scaled = back * gain
    return r * (scaled - n * jnp.mean(scaled * n, axis=-1, keepdims=True))


def ordered(first, own, other):
    return jnp.where(first, own, other), jnp.where(first, other, own)


def call(kernel, outs, flops=0, moved=8 << 20, name=None, vmem=VMEM_LIMIT, **kwargs):
    return pl.pallas_call(
        kernel,
        out_shape=[jax.ShapeDtypeStruct(shape, kind) for shape, kind in outs],
        compiler_params=pltpu.CompilerParams(vmem_limit_bytes=vmem),
        cost_estimate=pl.CostEstimate(flops=int(flops), bytes_accessed=moved, transcendentals=0),
        name=name,
        **kwargs,
    )


SMEM = pl.BlockSpec(memory_space=pltpu.SMEM)
VMEM = pl.BlockSpec(memory_space=pltpu.VMEM)


def whole(shape):
    return pl.BlockSpec(shape, lambda *i: (0,) * len(shape))


HALF = 80 + 20 + 10 + 2
PACKED = 2 * HALF + 80 + 40


def scale_kernel(x, ids, scaled):
    value = x[...]
    scaled[:TOK, :] = (value * norm_factor(value)).astype(BF)
    line = jnp.concatenate([ids[...].astype(F32), jnp.zeros((1, D - TOK), F32)], axis=1)
    scaled[TOK:, :] = jnp.broadcast_to(line, (16, D)).astype(BF)


def scale(x, ids):
    return call(scale_kernel, [((TOK + 16, D), BF)], name="scale")(x, ids)[0]


def pack_kernel(core, *refs):
    sources, (out, send, rows, *held, sems) = refs[:6], refs[6:]
    copies = [
        pltpu.make_async_copy(source, ref, sems.at[k])
        for k, (source, ref) in enumerate(zip(sources, held))
    ]
    for copy in copies:
        copy.start()
    gateup, query, keyval, down, output, gains = held
    first = core[0] == 0
    for copy in copies:
        copy.wait()
    gu = gateup[...]
    qs = query[...]
    kvs = keyval[...]
    rows[...] = jnp.zeros_like(rows)
    for t in range(16):
        part, x_at, yhi = t // 8, (t // 2) % 4, t % 2
        pair = []
        for c in range(2):
            at = [part * FF + (((x_at * 2 + ylo) * 2 + c) * 2 + yhi) * 64 for ylo in range(2)]
            pair.append(jnp.concatenate([gu[:, a : a + 64] for a in at], axis=1))
        for base, value in zip((0, HALF), ordered(first, *pair)):
            rows[base + 5 * t : base + 5 * t + 5, :] = value
    for t in range(6):
        if t < 4:
            pair = [qs[:, (c * 4 + t) * 128 : (c * 4 + t + 1) * 128] for c in range(2)]
        else:
            pair = [kvs[:, (c * 2 + t - 4) * 128 : (c * 2 + t - 3) * 128] for c in range(2)]
        for base, value in zip((80, HALF + 80), ordered(first, *pair)):
            rows[base + 5 * t : base + 5 * t + 5, :] = value
    for base, value in zip((110, HALF + 110), ordered(first, gains[0:1, :], gains[1:2, :])):
        rows[base : base + 1, :5] = value
    for t in range(5):
        at = 2 * HALF + t * 16
        rows[at : at + 16, :] = down[:, t * 128 : (t + 1) * 128]
        at = 2 * HALF + 80 + t * 8
        rows[at : at + 8, :] = output[:, t * 128 : (t + 1) * 128]
    out[:HALF, :] = rows[:HALF, :].astype(BF)
    out[HALF:, :] = rows[2 * HALF :, :].astype(BF)
    send[...] = rows[HALF : 2 * HALF, :].astype(BF)


def pack(core, gateup, query, keyval, down, output, gains):
    return call(
        pack_kernel,
        [((PACKED - HALF, 128), BF), ((HALF, 128), BF)],
        name="pack",
        vmem=60 * 1024 * 1024,
        in_specs=[SMEM] + [pl.BlockSpec(memory_space=pltpu.HBM)] * 6,
        scratch_shapes=[pltpu.VMEM((PACKED, 128), F32)]
        + [
            pltpu.VMEM(array.shape, F32)
            for array in (gateup, query, keyval, down, output, gains)
        ]
        + [pltpu.SemaphoreType.DMA((6,))],
    )(core, gateup, query, keyval, down, output, gains)


def layout_kernel(words, near, one, two, three, mlp, head, pieces, rows):
    first = words[0] == 0
    for step, ref in enumerate((near, one, two, three)):
        value = ref[...].astype(F32)
        halves = ordered(first, value[:HALF], value[PACKED - HALF :])
        pieces[lax.rem(words[2] + 4 - step, 4)] = jnp.concatenate(
            [*halves, value[HALF : PACKED - HALF]], axis=0
        )
    line = jnp.zeros((8, 128), F32)
    for z in range(4):
        for c in range(2):
            base = c * HALF
            for t in range(16):
                at = t * 40 + c * 20 + z * 5
                rows[at : at + 5, :] = pieces[z, base + 5 * t : base + 5 * t + 5, :]
            for t in range(6):
                at = ALL_ROWS + t * 40 + c * 20 + z * 5
                rows[at : at + 5, :] = pieces[z, base + 80 + 5 * t : base + 85 + 5 * t, :]
            gain = jnp.broadcast_to(pieces[z, base + 110 : base + 111, :], (8, 128))
            line += pltpu.roll(gain, c * 20 + z * 5, 1)
        for t in range(5):
            at = GU_ROWS + t * 64 + z * 16
            rows[at : at + 16, :] = pieces[z, 2 * HALF + 16 * t : 2 * HALF + 16 * t + 16, :]
            at = MLP_ROWS + t * 32 + z * 8
            rows[at : at + 8, :] = pieces[z, 2 * HALF + 80 + 8 * t : 2 * HALF + 88 + 8 * t, :]
    row = lax.broadcasted_iota(jnp.int32, (8, 128), 0)
    rows[ALL_ROWS + QKV_ROWS :, :] = jnp.where(row == 0, line, 0.0)
    mlp[...] = rows[:ALL_ROWS, :].astype(BF)
    head[...] = rows[ALL_ROWS:, :].astype(BF)


def lay_out(words, near, got):
    return call(
        layout_kernel,
        [((ALL_ROWS, 128), BF), ((FIRST_ROWS, 128), BF)],
        name="lay_out",
        in_specs=[SMEM] + [VMEM] * 4,
        scratch_shapes=[
            pltpu.VMEM((4, PACKED, 128), F32),
            pltpu.VMEM((ALL_ROWS + FIRST_ROWS, 128), F32),
        ],
    )(words, near, *got)


def wide_tiles(rows, tiles):
    return jnp.concatenate(
        [rows[:, t * 40 : (t + 1) * 40, :].reshape(D, 128) for t in range(tiles)], axis=1
    )


def tall_tiles(value, tiles):
    return jnp.concatenate(
        [value[:, t * 128 : (t + 1) * 128].reshape(16, 40, 128) for t in range(tiles)], axis=1
    )


def first_kernel(
    words, x, before, ids, own, other, swap, spread, keep, hidden, q, kv, wq, wkv, gains, gathered, row, column
):
    first = words[0] == 0
    own_ids = jnp.broadcast_to(ids[...].astype(F32), (8, TOK))
    old_ids = jnp.broadcast_to(before[TOK : TOK + 1, :TOK].astype(F32), (8, TOK))
    row[...] = jnp.concatenate([jnp.where(words[1] > 0, old_ids, -1.0), own_ids], axis=1)
    column[...] = own_ids.T

    def gain_row(ref):
        lanes = jnp.sum(ref[:, QKV_ROWS:, :].astype(F32), axis=1).astype(BF)
        return jnp.sum(mm(lanes, spread[...], NN) * keep[...], axis=0, keepdims=True)

    one, two = ordered(first, gain_row(own), gain_row(other))
    both = jnp.concatenate(
        [jnp.broadcast_to(one, (8, D)), jnp.broadcast_to(two, (8, D))], axis=0
    ).astype(BF)
    gathered[...] = both.astype(F32)
    both = mm(both, swap[...], NT)
    gains[...] = both
    value = x[...]
    value = jnp.concatenate([before[:TOK, :].astype(F32), value * norm_factor(value)], axis=0)
    h = (value * both[0:1]).astype(BF)
    h = mm(h, swap[...], NN).astype(BF)
    hidden[...] = h
    mine = wide_tiles(own[...], 6)
    theirs = wide_tiles(other[...], 6)
    w0, w1 = ordered(first, mine, theirs)
    weight = jnp.concatenate([w0[:, :512], w1[:, :512]], axis=1)
    wq[...] = weight
    q[...] = (mm(h[TOK:], weight, NN) * SCALE).astype(BF)
    weight = jnp.concatenate([w0[:, 512:], w1[:, 512:]], axis=1)
    wkv[...] = weight
    kv[...] = mm(h, weight, NN).astype(BF)


def project(words, x, before, ids, own, other, swap, spread, keep):
    outs = [
        ((2 * TOK, D), BF),
        ((TOK, 1024), BF),
        ((2 * TOK, 512), BF),
        ((D, 1024), BF),
        ((D, 512), BF),
        ((16, D), F32),
        ((16, D), F32),
        ((8, 2 * TOK), F32),
        ((TOK, 8), F32),
    ]
    specs = [SMEM] + [pl.BlockSpec(memory_space=pltpu.VMEM)] * 8
    return call(first_kernel, outs, 2 * TOK * D * 3400, name="project", in_specs=specs)(
        words, x, before, ids, own, other, swap, spread, keep
    )


QB = 128
BLOCKS = 2
SPAN = WINDOW + QB
ROW_PART = 64


def stacked(value):
    return jnp.concatenate([value[:, h * HD : (h + 1) * HD] for h in range(HQ)], axis=0)


def side_by_side(value):
    return jnp.concatenate([value[h * QB : (h + 1) * QB] for h in range(HQ)], axis=1)


def window_bias(ids, ids_all, step):
    at = pl.ds(pl.multiple_of(step * QB, QB), SPAN)
    key = lax.broadcasted_iota(jnp.int32, (QB, SPAN), 1)
    token = lax.broadcasted_iota(jnp.int32, (QB, SPAN), 0)
    seen = (key > token) & (key <= token + WINDOW) & (ids == ids_all[0:1, at])
    return jnp.where(seen, 0.0, MASKED)


def window_probs(q, keys, ids, ids_all, step):
    bias = window_bias(ids, ids_all, step)
    scores = mm(q, keys, NT) + jnp.concatenate([bias] * HQ, axis=0)
    exponent = jnp.exp(scores - jnp.max(scores, axis=-1, keepdims=True))
    return exponent / jnp.sum(exponent, axis=-1, keepdims=True)


def attend_kernel(q, both, ids, ids_all, out):
    for k in range(BLOCKS):
        block = pl.program_id(0) * BLOCKS + k
        rows = slice(k * QB, (k + 1) * QB)
        at = pl.ds(pl.multiple_of(block * QB, QB), SPAN)
        probs = window_probs(stacked(q[rows, :]), both[at, :HD], ids[rows, 0:1], ids_all, block)
        out[rows, :] = side_by_side(mm(probs.astype(BF), both[at, HD:], NN)).astype(BF)


def rows_of(width):
    return pl.BlockSpec((BLOCKS * QB, width), lambda i: (i, 0))


def attend(q, both, ids, ids_all):
    return call(
        attend_kernel,
        [((TOK, 1024), BF)],
        4 * TOK * HQ * SPAN * HD,
        name="attend",
        grid=(TOK // QB // BLOCKS,),
        in_specs=[rows_of(1024), VMEM, rows_of(8), VMEM],
        out_specs=[rows_of(1024)],
    )(q, both, ids, ids_all)[0]


def attend_back_kernel(q, back, both, ids, ids_all, dq, old, own, sums, scores, values, low_p, low_s):
    step = pl.program_id(0)

    @pl.when(step == 0)
    def _():
        sums[...] = jnp.zeros_like(sums)

    for k in range(BLOCKS):
        block = step * BLOCKS + k
        rows = slice(k * QB, (k + 1) * QB)
        at = pl.ds(pl.multiple_of(block * QB, QB), SPAN)
        keys = both[at, :HD]
        queries = stacked(q[rows, :])
        attended_back = stacked(back[rows, :])
        scores[k] = mm(queries, keys, NT)
        values[k] = mm(attended_back, both[at, HD:], NT)
        bias = window_bias(ids[rows, 0:1], ids_all, block)
        for first in range(0, HQ * QB, ROW_PART):
            part = slice(first, first + ROW_PART)
            token = first % QB
            raw = scores[k, part, :] + bias[token : token + ROW_PART]
            exponent = jnp.exp(raw - jnp.max(raw, axis=-1, keepdims=True))
            probs = exponent / jnp.sum(exponent, axis=-1, keepdims=True)
            prob_back = values[k, part, :]
            mean = jnp.sum(probs * prob_back, axis=-1, keepdims=True)
            low_p[k, part, :] = probs.astype(BF)
            low_s[k, part, :] = (probs * (prob_back - mean)).astype(BF)
        scores_back = low_s[k]
        dq[rows, :] = side_by_side(mm(scores_back, keys, NN) * SCALE).astype(BF)
        sums[at, :HD] += mm(scores_back.T, queries, NN)
        sums[at, HD:] += mm(low_p[k].T, attended_back, NN)

    @pl.when(step == TOK // QB // BLOCKS - 1)
    def _():
        old[...] = sums[:TOK, :].astype(BF)
        own[...] = sums[TOK:, :].astype(BF)


def attend_back(q, back, both, ids, ids_all):
    return call(
        attend_back_kernel,
        [((TOK, 1024), BF), ((TOK, 512), BF), ((TOK, 512), BF)],
        10 * TOK * HQ * SPAN * HD,
        name="attend_back",
        grid=(TOK // QB // BLOCKS,),
        in_specs=[
            rows_of(1024),
            rows_of(1024),
            VMEM,
            rows_of(8),
            VMEM,
        ],
        out_specs=[rows_of(1024), VMEM, VMEM],
        scratch_shapes=[
            pltpu.VMEM((2 * TOK, 512), F32),
            pltpu.VMEM((BLOCKS, HQ * QB, SPAN), F32),
            pltpu.VMEM((BLOCKS, HQ * QB, SPAN), F32),
            pltpu.VMEM((BLOCKS, HQ * QB, SPAN), BF),
            pltpu.VMEM((BLOCKS, HQ * QB, SPAN), BF),
        ],
    )(q, back, both, ids, ids_all)


def z_first():
    n = lax.broadcasted_iota(jnp.int32, (D, 128), 0)
    shard = (n * 205) >> 10
    z, yhi, core = shard & 3, (shard >> 2) & 1, (shard >> 3) & 1
    ylo, x = (shard >> 4) & 1, shard >> 5
    place = ((((z * 4 + x) * 2 + yhi) * 2 + ylo) * 2 + core) * 5 + n - 5 * shard
    column = lax.broadcasted_iota(jnp.int32, (D, 128), 1)
    tiles = [jnp.where(place == column + t * 128, 1.0, 0.0) for t in range(5)]
    return jnp.concatenate(tiles, axis=1).astype(BF)


def middle_kernel(x, attended, weights, gains, swap, cot, middle, h2, h2t, wo, db):
    w0, w1 = weights[0], weights[1]
    for x_at in range(4):
        for ylo in range(2):
            for c, rows in ((0, w0), (1, w1)):
                for yhi in range(2):
                    place = (x_at * 2 + yhi) * 2 + ylo
                    at = (((x_at * 2 + ylo) * 2 + c) * 2 + yhi) * 32
                    wo[at : at + 32, :] = jnp.concatenate(
                        [rows[place, t * 32 : (t + 1) * 32, :] for t in range(5)], axis=1
                    )
    value = x[...] + mm(attended[...], wo[...], NN)
    middle[...] = value
    h = (value * norm_factor(value) * gains[8:9, :]).astype(BF)
    h2[...] = mm(h, swap[...], NN).astype(BF)
    h2t[...] = mm(h, z_first(), NN).astype(BF).T
    db[...] = cot[...].astype(BF)


def to_middle(x, attended, weights, gains, swap, cot):
    outs = [((TOK, D), F32), ((TOK, D), BF), ((D, TOK), BF), ((1024, D), BF), ((TOK, D), BF)]
    return call(middle_kernel, outs, 2 * TOK * D * 1700, name="to_middle")(
        x, attended, weights, gains, swap, cot
    )


def middle_back_kernel(
    two, middle, h2, gains, gathered, cot, swap, wo, back, branch, attended_back, gain_sum
):
    two_back = natural_columns(two[...], swap[...])
    through = norm_back(two_back, middle[...], gains[8:9, :])
    terms = jnp.sum(two[...] * h2[...].astype(F32), axis=0, keepdims=True) / gathered[8:9, :]
    total = cot[...] + through
    back[...] = total
    branch[...] = total.astype(BF)
    attended_back[...] = mm(total.astype(BF), wo[...], NT).astype(BF)
    gain_sum[...] = jnp.broadcast_to(terms, (8, D))


def to_middle_back(two, middle, h2, gains, gathered, cot, swap, wo):
    outs = [((TOK, D), F32), ((TOK, D), BF), ((TOK, 1024), BF), ((8, D), F32)]
    return call(middle_back_kernel, outs, 2 * TOK * D * 2400, name="middle_back")(
        two, middle, h2, gains, gathered, cot, swap, wo
    )


def query_grad_kernel(core, dq, hidden, wq, attended, branch, own, other, one):
    first = core[0] == 0
    queries_back = dq[...]
    one[...] = mm(queries_back, wq[...], NT)
    sums = mm(hidden[TOK:, :].T, queries_back, NN).astype(BF)
    s_own, s_other = ordered(first, sums[:, :512], sums[:, 512:])
    own[:, :160, :] = tall_tiles(s_own, 4)
    other[:, :160, :] = tall_tiles(s_other, 4)
    sums = mm(attended[...].T, branch[...], NN).astype(BF)
    for x_at in range(4):
        for ylo in range(2):
            for yhi in range(2):
                place = (x_at * 2 + yhi) * 2 + ylo
                at = (((x_at * 2 + ylo) * 2) * 2 + yhi) * 32
                s_own, s_other = ordered(
                    first, sums[at : at + 32, :], sums[at + 64 : at + 96, :]
                )
                for t in range(5):
                    row = 160 + t * 32
                    own[place, row : row + 32, :] = s_own[:, t * 128 : (t + 1) * 128]
                    other[place, row : row + 32, :] = s_other[:, t * 128 : (t + 1) * 128]


def query_grad(core, dq, hidden, wq, attended, branch):
    outs = [((16, QO_ROWS, 128), BF), ((16, QO_ROWS, 128), BF), ((TOK, D), F32)]
    specs = [SMEM] + [pl.BlockSpec(memory_space=pltpu.VMEM)] * 5
    return call(
        query_grad_kernel, outs, 6 * TOK * D * 1024, name="query_grad", in_specs=specs
    )(core, dq, hidden, wq, attended, branch)


def last_kernel(core, old, kept, hidden, wkv, one, gathered, spread, keep, gain_two, own, other, total):
    first = core[0] == 0
    dkv = jnp.concatenate([old[...], kept[...]], axis=0)
    sums = mm(hidden[...].T, dkv, NN).astype(BF)
    s_own, s_other = ordered(first, sums[:, :256], sums[:, 256:])
    own[:, :80, :] = tall_tiles(s_own, 2)
    other[:, :80, :] = tall_tiles(s_other, 2)
    terms = mm(dkv, wkv[...], NT)
    one_own = one[...] + terms[TOK:]
    total[...] = one_own
    gain_sum = jnp.sum(one_own * hidden[TOK:, :].astype(F32), axis=0, keepdims=True)
    gain_sum += jnp.sum(terms[:TOK] * hidden[:TOK, :].astype(F32), axis=0, keepdims=True)
    g_own, g_other = ordered(first, gain_sum / gathered[0:1, :], gain_two[0:1, :])
    row = lax.broadcasted_iota(jnp.int32, (16, 16, 128), 1)
    for ref, line in ((own, g_own), (other, g_other)):
        lanes = mm((keep[...] * line).astype(BF), spread[...], NT)
        ref[:, 80:, :] = jnp.where(row == 0, lanes[:, None, :], 0.0).astype(BF)


def last_grad(core, old, kept, hidden, wkv, one, gathered, spread, keep, gain_two):
    outs = [((16, KV_ROWS, 128), BF), ((16, KV_ROWS, 128), BF), ((TOK, D), F32)]
    return call(
        last_kernel,
        outs,
        2 * TOK * D * 2100,
        name="last_grad",
        in_specs=[SMEM] + [pl.BlockSpec(memory_space=pltpu.VMEM)] * 9,
    )(core, old, kept, hidden, wkv, one, gathered, spread, keep, gain_two)


def input_kernel(one, came_back, wkv, swap, x, gains, middle_back, grad):
    one_back = natural_columns(one[...] + mm(came_back[...], wkv[...], NT), swap[...])
    grad[...] = middle_back[...] + norm_back(one_back, x[...], gains[0:1, :])


def to_input(one, came_back, wkv, swap, x, gains, middle_back):
    return call(input_kernel, [((TOK, D), F32)], 2 * TOK * D * 1800, name="to_input")(
        one, came_back, wkv, swap, x, gains, middle_back
    )[0]


NEAR_ROWS = 32 + 32 + 40


def order_kernel(part, out, rows, moved):
    rows[...] = part[:Z_GU, :].astype(F32)
    for place in range(16):
        for t in range(16):
            at = t * 160 + place * 10
            moved[place, t * 10 : t * 10 + 10, :] = rows[at : at + 10, :]
    out[:, :160, :] = moved[...].astype(BF)
    out[:, 160:, :] = part[Z_GU:, :].reshape(16, 80, 128)


def places_first(part):
    return call(
        order_kernel,
        [((16, FAR_ROWS, 128), BF)],
        name="places_first",
        scratch_shapes=[pltpu.VMEM((Z_GU, 128), F32), pltpu.VMEM((16, 160, 128), F32)],
    )(part)[0]


def parts_kernel(words, firsts, kept, *refs):
    *sends, rows, head = refs
    first = words[0] == 0
    head[...] = jnp.sum(firsts[...].astype(F32), axis=0)
    for z in range(4):
        for c in range(2):
            base = c * 32
            for t in range(6):
                at = (t * 40 if t < 4 else QO_ROWS + (t - 4) * 40) + c * 20 + z * 5
                rows[z, base + 5 * t : base + 5 * t + 5, :] = head[at : at + 5, :]
            lanes = pltpu.roll(head[QO_ROWS + 80 : QO_ROWS + 88, :], (128 - c * 20 - z * 5) % 128, 1)
            rows[z, base + 30 : base + 32, :] = lanes[0:2, :]
        for t in range(5):
            at = 160 + t * 32 + z * 8
            rows[z, 64 + t * 8 : 72 + t * 8, :] = head[at : at + 8, :]
    for step, ref in enumerate((kept, *sends)):
        value = rows[lax.rem(words[2] + step, 4)]
        halves = ordered(first, value[:32], value[32:64])
        ref[...] = jnp.concatenate([*halves, value[64:]], axis=0).astype(ref.dtype)


def near_parts(words, firsts):
    return call(
        parts_kernel,
        [((NEAR_ROWS, 128), F32)] + [((NEAR_ROWS, 128), BF)] * 3,
        name="near_parts",
        in_specs=[SMEM, pl.BlockSpec(memory_space=pltpu.VMEM)],
        scratch_shapes=[
            pltpu.VMEM((4, NEAR_ROWS, 128), F32),
            pltpu.VMEM((QO_ROWS + KV_ROWS, 128), F32),
        ],
    )(words, firsts)


def total_kernel(words, kept, one, two, three, parts, own, send, rows, halves):
    first = words[0] == 0
    near = kept[...] + sum(ref[...].astype(F32) for ref in (one, two, three))
    rows[...] = jnp.sum(parts[...].astype(F32), axis=0)
    for c in range(2):
        for t in range(16):
            at = t * 10 + c * 5
            halves[c, t * 5 : t * 5 + 5, :] = rows[at : at + 5, :]
    mine, theirs = ordered(first, halves[0], halves[1])
    own[...] = jnp.concatenate([mine, near[:32], rows[160:, :], near[64:]], axis=0)
    send[...] = jnp.concatenate([theirs, near[32:64]], axis=0).astype(BF)


def near_total(words, kept, got, parts):
    outs = [((PACKED - HALF, 128), F32), ((HALF, 128), BF)]
    return call(
        total_kernel,
        outs,
        name="near_total",
        in_specs=[SMEM] + [pl.BlockSpec(memory_space=pltpu.VMEM)] * 5,
        scratch_shapes=[pltpu.VMEM((FAR_ROWS, 128), F32), pltpu.VMEM((2, 80, 128), F32)],
    )(words, kept, *got, parts)


def adamw_kernel(words, own, got, *refs):
    olds, news = refs[:18], refs[18:]
    first = words[0] == 0
    halves = ordered(first, own[:HALF, :], got[...].astype(F32))
    pieces = []
    for part in range(2):
        for x_at in range(4):
            for ylo in range(2):
                for c in range(2):
                    pair = [5 * ((part * 4 + x_at) * 2 + yhi) for yhi in range(2)]
                    pieces += [halves[c][a : a + 5, ylo * 64 : ylo * 64 + 64] for a in pair]
    gateup = jnp.concatenate(pieces, axis=1)
    query = [halves[c][80 + 5 * t : 85 + 5 * t] for c in range(2) for t in range(4)]
    keyval = [halves[c][100 + 5 * t : 105 + 5 * t] for c in range(2) for t in range(2)]
    down = [own[HALF + 16 * t : HALF + 16 * t + 16, :] for t in range(5)]
    output = [own[HALF + 80 + 8 * t : HALF + 88 + 8 * t, :] for t in range(5)]
    gains = jnp.concatenate([halves[c][110:111, :5] for c in range(2)], axis=0)
    rate = RATE_FACTOR * D ** (-0.5)
    steps = (
        (jnp.concatenate(query, axis=1), rate, DECAY),
        (jnp.concatenate(keyval, axis=1), rate, DECAY),
        (jnp.concatenate(output, axis=1), RATE_FACTOR * (HQ * HD // WINDOW) ** (-0.5), DECAY),
        (gateup, rate, DECAY),
        (jnp.concatenate(down, axis=1), RATE_FACTOR * FF ** (-0.5), DECAY),
        (gains, GAIN_RATE, 0.0),
    )
    for k, (gradient, rate, decay) in enumerate(steps):
        weight, mean, square = (ref[...] for ref in olds[3 * k : 3 * k + 3])
        new = adamw_step(weight, mean, square, gradient, rate, decay)
        for ref, value in zip(news[3 * k : 3 * k + 3], new):
            ref[...] = value


def adamw_all(words, own, got, arrays):
    outs = [(arrays[3 * k].shape, F32) for k in range(6) for _ in range(3)]
    return call(
        adamw_kernel,
        outs,
        name="adamw",
        vmem=60 * 1024 * 1024,
        in_specs=[SMEM] + [pl.BlockSpec(memory_space=pltpu.VMEM)] * 20,
    )(words, own, got, *arrays)


GELU_K = 0.7978845608028654
GELU_A = 0.044715
STEP_TILES = 2
FF_STEPS = 8 // STEP_TILES


def mlp_kernel(which, h2, h2t, db, gate_w, up_w, down_w, *refs):
    del which
    *sums_in, out, two, grads, gates, ups, inner_backs, inners, gate_backs, up_backs = refs
    step = pl.program_id(0)
    n = STEP_TILES

    @pl.when(step == 0)
    def _():
        out[...] = sums_in[0][...]
        two[...] = sums_in[1][...] if len(sums_in) > 1 else jnp.zeros_like(two)

    wg = wide_tiles(gate_w[...], n)
    wu = wide_tiles(up_w[...], n)
    wd = jnp.concatenate(
        [
            jnp.concatenate([down_w[c, t * 64 : (t + 1) * 64, :] for t in range(5)], axis=1)
            for c in range(2 * n)
        ],
        axis=0,
    )
    hidden = h2[...]
    back = db[...]
    gates[...] = mm(hidden, wg, NN)
    ups[...] = mm(hidden, wu, NN)
    inner_backs[...] = mm(back, wd, NT)
    for first in range(0, TOK, ROW_PART):
        part = slice(first, first + ROW_PART)
        gate, up, inner_back = gates[part, :], ups[part, :], inner_backs[part, :]
        square = gate * gate
        half = 0.5 + 0.5 * jnp.tanh(gate * (GELU_K + GELU_K * GELU_A * square))
        gelu = gate * half
        slope = half + (gelu - gelu * half) * (2.0 * GELU_K + 6.0 * GELU_K * GELU_A * square)
        inners[part, :] = (gelu * up).astype(BF)
        gate_backs[part, :] = (inner_back * up * slope).astype(BF)
        up_backs[part, :] = (inner_back * gelu).astype(BF)
    inner, gate_back, up_back = inners[...], gate_backs[...], up_backs[...]
    out[...] += mm(inner, wd, NN)
    two[...] += mm(gate_back, wg, NT) + mm(up_back, wu, NT)
    dg = mm(h2t[...], gate_back, ((1,), (0,))).astype(BF)
    du = mm(h2t[...], up_back, ((1,), (0,))).astype(BF)
    dd = mm(inner.T, back, NN).astype(BF)
    for t in range(n):
        lanes = slice(t * 128, (t + 1) * 128)
        at = pl.multiple_of((step * n + t) * 160, 160)
        grads[:, pl.ds(at, 160), :] = dg[:, lanes].reshape(4, 160, 128)
        grads[:, pl.ds(Z_GU // 2 + at, 160), :] = du[:, lanes].reshape(4, 160, 128)
        for ylo in range(2):
            at = pl.multiple_of(Z_GU + ((step * n + t) * 2 + ylo) * 80, 80)
            for z in range(4):
                part = dd[t * 128 + ylo * 64 + z * 16 : t * 128 + ylo * 64 + z * 16 + 16, :]
                grads[z, pl.ds(at, 80), :] = jnp.concatenate(
                    [part[:, k * 128 : (k + 1) * 128] for k in range(5)], axis=0
                )


def mlp_half(which, h2, h2t, db, weights, *sums_in):
    n = STEP_TILES
    return pl.pallas_call(
        mlp_kernel,
        grid_spec=pltpu.PrefetchScalarGridSpec(
            num_scalar_prefetch=1,
            grid=(FF_STEPS,),
            in_specs=[
                VMEM,
                VMEM,
                VMEM,
                pl.BlockSpec((None, 16, n * 40, 128), lambda i, w: (w[0], 0, i, 0)),
                pl.BlockSpec((None, 16, n * 40, 128), lambda i, w: (w[0], 0, FF_STEPS + i, 0)),
                pl.BlockSpec((None, 2 * n, DOWN_ROWS, 128), lambda i, w: (w[0], i, 2, 0)),
            ]
            + [VMEM] * len(sums_in),
            out_specs=[VMEM, VMEM, VMEM],
            scratch_shapes=[pltpu.VMEM((TOK, n * 128), F32)] * 3
            + [pltpu.VMEM((TOK, n * 128), BF)] * 3,
        ),
        out_shape=[
            jax.ShapeDtypeStruct((TOK, D), F32),
            jax.ShapeDtypeStruct((TOK, D), F32),
            jax.ShapeDtypeStruct((4, Z_ROWS, 128), BF),
        ],
        compiler_params=pltpu.CompilerParams(vmem_limit_bytes=MLP_VMEM),
        cost_estimate=pl.CostEstimate(
            flops=18 * TOK * D * 1024, bytes_accessed=16 << 20, transcendentals=TOK * 1024
        ),
        name="mlp_half",
    )(which, h2, h2t, db, weights, weights, weights, *sums_in)


def local(
    block_in,
    seg_ids,
    cotangent,
    query_weight,
    query_mean,
    query_square,
    keyval_weight,
    keyval_mean,
    keyval_square,
    output_weight,
    output_mean,
    output_square,
    gateup_weight,
    gateup_mean,
    gateup_square,
    down_weight,
    down_mean,
    down_square,
    norm_gains,
    gains_mean,
    gains_square,
):
    tokens_in = block_in[0]
    core = lax.axis_index("core")
    core_word = core.reshape(1).astype(jnp.int32)
    spread, keep = (jnp.asarray(part) for part in gain_rows())
    spread = spread.astype(BF)

    swap = jnp.asarray(gathered_rows(), BF)
    has_before = (lax.axis_index(SEQ) > 0).astype(jnp.int32)
    words = jnp.stack([core.astype(jnp.int32), has_before, lax.axis_index("z").astype(jnp.int32)])

    mine, send = pack(
        core_word, gateup_weight, query_weight, keyval_weight, down_weight, output_weight, norm_gains
    )
    near = jnp.concatenate([mine, other_core(send)], axis=0)
    got = [sent_z(near, step) for step in (1, 2, 3)]
    mlp_block, first_block = lay_out(words, near, got)

    weights = lax.all_gather(mlp_block, ("core",) + FAR, axis=0, tiled=False)
    weights = weights.reshape(2, 16, ALL_ROWS, 128)
    first_block, scaled = lax.optimization_barrier((first_block, scale(tokens_in, seg_ids)))
    before = lax.ppermute(scaled, SEQ, [(i, i + 1) for i in range(15)])
    first_own = lax.all_gather(first_block, FAR, axis=0, tiled=False)
    first_own, before = lax.optimization_barrier((first_own, before))
    first_other = other_core(first_own)
    upstream = cotangent[0]

    hidden_one, queries, keyvals, wq, wkv, gains_all, gains_gathered, ids_all, ids = project(
        words, tokens_in, before, seg_ids, first_own, first_other, swap, spread, keep
    )
    attended = attend(queries, keyvals, ids, ids_all)

    weights, attended = lax.optimization_barrier((weights, attended))
    middle, hidden_two, hidden_two_t, wo, down_back = to_middle(
        tokens_in, attended, weights[:, :, MLP_ROWS:], gains_all, swap, upstream
    )
    out_part, two_part, grads_other = mlp_half(
        1 - core_word, hidden_two, hidden_two_t, down_back, weights, middle
    )
    grads_there = other_core(grads_other)
    block_out, two_back, grads_own = mlp_half(
        core_word, hidden_two, hidden_two_t, down_back, weights, out_part, two_part
    )
    grads_both = (grads_own.astype(F32) + grads_there.astype(F32)).astype(BF)
    mlp_part = lax.psum_scatter(
        grads_both.reshape(4 * Z_ROWS, 128), "z", scatter_dimension=0, tiled=True
    )

    middle_back, branch_back, attended_back, gain_two_sum = to_middle_back(
        two_back, middle, hidden_two, gains_all, gains_gathered, upstream, swap, wo
    )
    queries_back, old_back, kept_back = attend_back(queries, attended_back, keyvals, ids, ids_all)
    came_back = lax.ppermute(old_back, SEQ, [(i + 1, i) for i in range(15)])
    qo_own, qo_other, one_part = query_grad(
        core_word, queries_back, hidden_one, wq, attended, branch_back
    )
    qo_there = other_core(qo_other)
    kv_own, kv_other, one_part = last_grad(
        core_word,
        old_back,
        kept_back,
        hidden_one,
        wkv,
        one_part,
        gains_gathered,
        spread,
        keep,
        gain_two_sum,
    )
    kv_there = other_core(kv_other)
    sums_both = jnp.concatenate(
        [
            (mine.astype(F32) + there.astype(F32)).astype(BF)
            for mine, there in ((qo_own, qo_there), (kv_own, kv_there))
        ],
        axis=1,
    )
    first_part = lax.all_to_all(sums_both, FAR, 0, 0, tiled=True)
    moved, came_back = lax.optimization_barrier((places_first(mlp_part), came_back))
    mlp_far = lax.all_to_all(moved, FAR, 0, 0, tiled=True)

    kept, *sends = near_parts(words, first_part)
    kept, came_back = lax.optimization_barrier((kept, came_back))
    input_grad = to_input(one_part, came_back, wkv, swap, tokens_in, gains_all, middle_back)
    kept, input_grad = lax.optimization_barrier((kept, input_grad))
    own_sum, other_sum = near_total(
        words, kept, [sent_z(sends[k], k + 1) for k in range(3)], mlp_far
    )
    news = adamw_all(
        words,
        own_sum,
        other_core(other_sum),
        (
            query_weight,
            query_mean,
            query_square,
            keyval_weight,
            keyval_mean,
            keyval_square,
            output_weight,
            output_mean,
            output_square,
            gateup_weight,
            gateup_mean,
            gateup_square,
            down_weight,
            down_mean,
            down_square,
            norm_gains,
            gains_mean,
            gains_square,
        ),
    )
    return (block_out[None], input_grad[None], *news)


def solution(mesh):
    fine = Mesh(mesh.devices.reshape([SIZES[a] for a in OWNERS]), OWNERS)
    tokens = P(("yhi", "z"), SEQ, None)
    rows = P(OWNERS, None)
    columns = P(None, OWNERS)
    return jax.shard_map(
        local,
        mesh=fine,
        in_specs=(tokens, P(("yhi", "z"), SEQ), tokens) + (rows,) * 15 + (columns,) * 3,
        out_specs=(tokens, tokens) + (rows,) * 15 + (columns,) * 3,
        check_vma=False,
    )
```
